32 devices in a mesh: rep: 16 (over z, x, core), tp: 2 (over y).
Axes of the slice: x: 2, y: 2, z: 4, core: 2. Of those that a mesh axis runs over, the one named last changes fastest.
Arguments:
- inputs: bfloat16 [16, 1, 128, 5120], P('rep', None, None, 'tp'), may hold values from -6 to 6
- out_grads: bfloat16 [16, 1, 128, 5120], P('rep', None, None, 'tp'), may hold values from -6 to 6
- weights: float32 [16, 3, 10, 5120], P('rep', None, 'tp'), may hold values from -0.078125 to 0.078125
- first_moment: float32 [16, 3, 10, 5120], P('rep', None, 'tp'), may hold values from -0.006 to 0.006
- second_moment: float32 [16, 3, 10, 5120], P('rep', None, 'tp'), may hold values from 1e-07 to 1e-05
- partners: int32 [1, 16], replicated, may hold values from 0 to 15, as said below
Outputs:
- new_weights: float32 [16, 3, 10, 5120], P('rep', None, 'tp')
- new_first: float32 [16, 3, 10, 5120], P('rep', None, 'tp')
- new_second: float32 [16, 3, 10, 5120], P('rep', None, 'tp')
The draws below stay inside these ranges and needn't reach their ends.
Inputs may be any that keep to these rules, and one draw needn't show every extreme that they name: For each step s there is a nonzero constant c such that partners[s, i] = i XOR c for every group i; 16 is a power of two.
All inputs are finite; a program needn't handle non-finite values.
Results may differ from the reference program's by a relative error of at most 0.0016.
Values may be sent and summed in bfloat16 or wider, within the bound.
A program may use at most 64 MiB of HBM per device.

```python
import math
import jax
import jax.numpy as jnp
from jax import lax

D = 5120
TOK = 128
STEPS = 1
STEP0 = 1000
GROUPS = 16
HID = 10


def draw_partners(key, part):
    key = jax.random.fold_in(key, 7)
    masks = jax.random.randint(key, (STEPS, 1), 1, GROUPS, dtype=jnp.int32)
    groups = jnp.arange(GROUPS, dtype=jnp.int32)[None, :]
    return jnp.bitwise_xor(groups, masks).astype(jnp.int32)


def steps_of(key, shape, split, least, largest):
    level = 1.0
    for axis_at, blocks in split:
        heights = jax.random.uniform(jax.random.fold_in(jax.random.fold_in(key, 6), axis_at), (blocks,), jnp.float32, least / len(split), largest / len(split))
        level = level * jnp.repeat(jnp.exp(heights), shape[axis_at] // blocks).reshape((-1,) + (1,) * (len(shape) - 1 - axis_at))
    return level


def normal_values(key, dims, deviation, reach, cuts=(), kind=jnp.bfloat16):
    entries = deviation * jax.random.normal(key, dims, jnp.float32)
    if cuts:
        entries = entries * steps_of(key, dims, cuts, -0.22, 0.18)
    return jnp.clip(entries, -reach, reach).astype(kind)


def setup_inputs(seed: int = 0) -> dict:
    seeds = jax.random.split(jax.random.key(seed), 7)
    return {
        "inputs": normal_values(seeds[0], (GROUPS, STEPS, TOK, D), 1.0, 6.0, ((0, 16), (3, 2))),
        "out_grads": normal_values(seeds[1], (GROUPS, STEPS, TOK, D), 1.0, 6.0, ((0, 16), (3, 2))),
        "weights": normal_values(seeds[2], (GROUPS, 3, HID, D), D ** -0.5, 0.078125, ((0, 16), (2, 2)), jnp.float32),
        "first_moment": normal_values(seeds[3], (GROUPS, 3, HID, D), 0.001, 0.006, ((0, 16), (2, 2)), jnp.float32),
        "second_moment": jnp.clip(jnp.exp(math.log(9.999999747378752e-06) - 4.6051701 * jax.random.uniform(seeds[4], (GROUPS, 3, HID, D), jnp.float32) ** steps_of(seeds[4], (GROUPS, 3, HID, D), ((0, 16), (2, 2)), -0.2, 0.2)), 1.0000000116860974e-07, 9.999999747378752e-06),
        "partners": draw_partners(jax.random.fold_in(seeds[6], 71), 0),
    }


CLIP = 1.0
BETA1 = 0.9
BETA2 = 0.95
LEARN = 0.001
DECAY = 0.1
EPSILON = 1e-08

def reference(inputs, out_grads, weights, first_moment, second_moment, partners):
    params, first, second = (weights, first_moment, second_moment)
    for step in range(STEPS):
        tokens = inputs[:, step].astype(jnp.float32)
        cotan = out_grads[:, step].astype(jnp.float32)
        low = lax.optimization_barrier(params.astype(jnp.bfloat16)).astype(jnp.float32)
        gate = jnp.einsum('gtd,ghd->gth', tokens, low[:, 0])
        upper = jnp.einsum('gtd,ghd->gth', tokens, low[:, 1])
        back = jnp.einsum('gtd,ghd->gth', cotan, low[:, 2])
        sig = jax.nn.sigmoid(gate)
        hidden = lax.optimization_barrier((gate * sig * upper).astype(jnp.bfloat16)).astype(jnp.float32)
        d_up = lax.optimization_barrier((back * gate * sig).astype(jnp.bfloat16)).astype(jnp.float32)
        d_gate = lax.optimization_barrier((back * upper * sig * (1.0 + gate * (1.0 - sig))).astype(jnp.bfloat16)).astype(jnp.float32)
        grads = jnp.stack([jnp.einsum('gth,gtd->ghd', d_gate, tokens), jnp.einsum('gth,gtd->ghd', d_up, tokens), jnp.einsum('gth,gtd->ghd', hidden, cotan)], axis=1)
        norm = jnp.sqrt(lax.optimization_barrier(jnp.sum(grads * grads, axis=(1, 2, 3), keepdims=True)))
        clipped = grads * (CLIP / jnp.maximum(norm, CLIP))
        count = STEP0 + step + 1
        fix_one = 1.0 - BETA1 ** count
        fix_two = 1.0 - BETA2 ** count
        first = BETA1 * first + (1.0 - BETA1) * clipped
        second = BETA2 * second + (1.0 - BETA2) * clipped * clipped
        params = params - LEARN * (first / fix_one / (jnp.sqrt(second / fix_two) + EPSILON) + DECAY * params)
        mate = partners[step]
        params = 0.5 * (params + params[mate])
        first = 0.5 * (first + first[mate])
        second = 0.5 * (second + second[mate])
    return (params, first, second)
```

```python
import functools

import jax
import jax.numpy as jnp
from jax import lax
from jax.experimental import pallas as pl
from jax.experimental.pallas import tpu as pltpu
from jax.sharding import PartitionSpec as P

STEP0 = 1000
CLIP = 1.0
BETA1 = 0.9
BETA2 = 0.95
LEARN = 0.001
DECAY = 0.1
EPSILON = 1e-08
COUNT = STEP0 + 1
FIX_ONE = 1.0 - BETA1**COUNT
FIX_TWO = 1.0 - BETA2**COUNT

MESH = pl.DeviceIdType.MESH
BF16 = jnp.bfloat16
F32 = jnp.float32
LANE = 128


def flipped(index, mask):
    out = index
    bit = 1
    while bit <= mask:
        if mask & bit:
            out = out + bit * (1 - 2 * ((index // bit) % 2))
        bit *= 2
    return out


def adamw(params, first, second, grads, scale):
    clipped = grads * scale
    first = BETA1 * first + (1.0 - BETA1) * clipped
    second = BETA2 * second + (1.0 - BETA2) * clipped * clipped
    step = first * (1.0 / FIX_ONE) / (jnp.sqrt(second * (1.0 / FIX_TWO)) + EPSILON)
    params = params - LEARN * (step + DECAY * params)
    return params, first, second


def kernel(
    n_tp, mask, rows,
    x_ref, dy_ref, w_ref, m_ref, v_ref,
    ow_ref, om_ref, ov_ref,
    xy, raw, packed, low, mate, lowall, part, sums, deriv,
    gsend, gall, gmate, sq, sqall, sqsum, sqmate, result, outs,
    load_sem, store_sem,
    low_send, low_recv, part_send, part_recv, g_send, g_recv, sq_send, sq_recv,
    early_send, early_recv, fwd_send, fwd_recv, sqm_send, sqm_recv,
):
    rep = lax.axis_index("rep")
    tp = lax.axis_index("tp")
    partner = flipped(rep, mask)
    tok = x_ref.shape[2]
    feat = x_ref.shape[3]
    width = w_ref.shape[3]
    depth = packed.shape[1]
    used = 3 * rows

    loads = [
        pltpu.make_async_copy(w_ref.at[0], raw.at[0], load_sem.at[0]),
        pltpu.make_async_copy(x_ref.at[0, 0], xy.at[pl.ds(0, tok)], load_sem.at[1]),
        pltpu.make_async_copy(dy_ref.at[0, 0], xy.at[pl.ds(tok, tok)], load_sem.at[2]),
        pltpu.make_async_copy(m_ref.at[0], raw.at[1], load_sem.at[3]),
        pltpu.make_async_copy(v_ref.at[0], raw.at[2], load_sem.at[4]),
    ]
    for load in loads:
        load.start()

    barrier = pltpu.get_barrier_semaphore()
    peers = [lax.rem(tp + d, n_tp) for d in range(1, n_tp)]
    sources = [lax.rem(tp + n_tp - d, n_tp) for d in range(1, n_tp)]
    for peer in peers:
        pl.semaphore_signal(barrier, inc=1, device_id={"tp": peer}, device_id_type=MESH)
    pl.semaphore_signal(barrier, inc=1, device_id={"rep": partner}, device_id_type=MESH)

    def to_peer(src, dst, send, recv, peer):
        return pltpu.make_async_remote_copy(
            src_ref=src, dst_ref=dst, send_sem=send, recv_sem=recv,
            device_id={"tp": peer}, device_id_type=MESH,
        )

    def to_mate(src, dst, send, recv):
        return pltpu.make_async_remote_copy(
            src_ref=src, dst_ref=dst, send_sem=send, recv_sem=recv,
            device_id={"rep": partner}, device_id_type=MESH,
        )

    def columns(block):
        return pl.ds(pl.multiple_of(block * feat, LANE), feat)

    def pack(which):
        for k in range(3):
            packed[which, pl.ds(k * rows, rows), :] = raw[which, k]
        if used < depth:
            packed[which, pl.ds(used, depth - used), :] = jnp.zeros((depth - used, width), F32)
        low[which] = packed[which].astype(BF16)

    loads[0].wait()
    pack(0)
    pl.semaphore_wait(barrier, n_tp)
    low_copies = [
        to_peer(low.at[0, :, columns(peer)], lowall.at[tp], low_send.at[d], low_recv.at[d], peer)
        for d, peer in enumerate(peers)
    ]
    for copy in low_copies:
        copy.start()
    early = [to_mate(low.at[k], mate.at[k], early_send.at[k], early_recv.at[k]) for k in range(3)]
    early[0].start()
    lowall[tp] = low[0, :, columns(tp)]
    loads[3].wait()
    pack(1)
    early[1].start()
    loads[4].wait()
    pack(2)
    early[2].start()

    loads[1].wait()
    loads[2].wait()
    for copy in low_copies:
        copy.wait_recv()
    prod = lax.dot_general(
        lowall[...].reshape(n_tp * depth, feat), xy[...],
        (((1,), (1,)), ((), ())), preferred_element_type=F32,
    ).reshape(n_tp, depth, 2 * tok)
    row = lax.broadcasted_iota(jnp.int32, (n_tp, depth, tok), 1)
    part[tp] = jnp.where(row < 2 * rows, prod[:, :, :tok], prod[:, :, tok:])
    part_copies = [
        to_peer(part.at[tp], part.at[tp], part_send.at[d], part_recv.at[d], peer)
        for d, peer in enumerate(peers)
    ]
    for copy in part_copies:
        copy.start()
    for copy in part_copies:
        copy.wait_recv()
    total = part[0]
    for t in range(1, n_tp):
        total = total + part[t]
    sums[...] = total
    gate = sums[:, pl.ds(0, rows), :]
    upper = sums[:, pl.ds(rows, rows), :]
    back = sums[:, pl.ds(2 * rows, rows), :]
    sig = jax.nn.sigmoid(gate)
    hidden = (gate * sig * upper).astype(BF16).astype(F32)
    d_up = (back * gate * sig).astype(BF16).astype(F32)
    d_gate = (back * upper * sig * (1.0 + gate * (1.0 - sig))).astype(BF16).astype(F32)
    deriv[:, pl.ds(0, rows), :] = d_gate
    deriv[:, pl.ds(rows, rows), :] = d_up
    deriv[:, pl.ds(2 * rows, rows), :] = hidden
    if used < depth:
        deriv[:, pl.ds(used, depth - used), :] = jnp.zeros((n_tp, depth - used, tok), F32)
    both = deriv[...]
    left = jnp.concatenate(
        [jnp.where(row < 2 * rows, both, 0.0), jnp.where(row < 2 * rows, 0.0, both)], axis=2
    ).astype(BF16).reshape(n_tp * depth, 2 * tok)
    grads = jnp.dot(left, xy[...], preferred_element_type=F32)
    gsend[...] = grads.astype(BF16).reshape(n_tp, depth, feat)
    g_copies = [
        to_peer(gsend.at[peer], gall.at[tp], g_send.at[d], g_recv.at[d], peer)
        for d, peer in enumerate(peers)
    ]
    for copy in g_copies:
        copy.start()
    own = to_mate(gsend.at[tp], gmate.at[tp], fwd_send.at[n_tp - 1], fwd_recv.at[n_tp - 1])
    own.start()
    sq[...] = jnp.broadcast_to(jnp.sum(grads * grads, keepdims=True), sq.shape)
    sqall[tp] = sq[...]
    sq_copies = [
        to_peer(sq, sqall.at[tp], sq_send.at[d], sq_recv.at[d], peer)
        for d, peer in enumerate(peers)
    ]
    for copy in sq_copies:
        copy.start()
    gall[tp] = gsend[tp]

    forwards = []
    for d, source in enumerate(sources):
        g_copies[d].wait_recv()
        copy = to_mate(gall.at[source], gmate.at[source], fwd_send.at[d], fwd_recv.at[d])
        copy.start()
        forwards.append(copy)
    for copy in sq_copies:
        copy.wait_recv()
    square = sqall[0]
    for t in range(1, n_tp):
        square = square + sqall[t]
    sqsum[...] = square
    sq_mate = to_mate(sqsum, sqmate, sqm_send.at[0], sqm_recv.at[0])
    sq_mate.start()
    scale = CLIP / jnp.maximum(jnp.sqrt(square), CLIP)

    def column_loop(body):
        step = feat if feat <= 640 else 640
        for block in range(n_tp):
            @pl.loop(0, feat // step)
            def _(i):
                for j in range(step // LANE):
                    at = pl.multiple_of(i * step, LANE) + j * LANE
                    body(block, pl.ds(pl.multiple_of(at, LANE), LANE),
                         pl.ds(pl.multiple_of(at + block * feat, LANE), LANE))

    factor = jnp.concatenate([scale] * (depth // 8), axis=0)

    def own_update(block, inner, outer):
        new = adamw(
            packed[0, :, outer], packed[1, :, outer], packed[2, :, outer],
            gall[block, :, inner].astype(F32), factor,
        )
        for k in range(3):
            packed[k, :, outer] = new[k]

    column_loop(own_update)

    for copy in early:
        copy.wait_recv()
    own.wait_recv()
    for copy in forwards:
        copy.wait_recv()
    sq_mate.wait_recv()
    mate_scale = CLIP / jnp.maximum(jnp.sqrt(sqmate[...]), CLIP)
    mate_factor = jnp.concatenate([mate_scale] * (depth // 8), axis=0)

    def mate_update(block, inner, outer):
        new = adamw(
            mate[0, :, outer].astype(F32), mate[1, :, outer].astype(F32),
            mate[2, :, outer].astype(F32), gmate[block, :, inner].astype(F32), mate_factor,
        )
        for k in range(3):
            result[k, :, outer] = 0.5 * (packed[k, :, outer] + new[k])

    column_loop(mate_update)
    stores = []
    for which, ref in enumerate((ow_ref, om_ref, ov_ref)):
        for k in range(3):
            outs[which, k] = result[which, pl.ds(k * rows, rows), :]
        store = pltpu.make_async_copy(outs.at[which], ref.at[0], store_sem.at[which])
        store.start()
        stores.append(store)
    for copy in low_copies + part_copies + g_copies + sq_copies + early + forwards + [own, sq_mate]:
        copy.wait_send()
    for store in stores:
        store.wait()


def exchange(n_tp, mask, x, dy, w, m, v):
    _, _, tok, feat = x.shape
    _, _, rows, width = w.shape
    depth = -(-3 * rows // 16) * 16
    dma = pltpu.SemaphoreType.DMA
    hbm = pl.BlockSpec(memory_space=pl.ANY)
    many = (max(n_tp - 1, 1),)
    state = jax.ShapeDtypeStruct(w.shape, F32)
    return pl.pallas_call(
        functools.partial(kernel, n_tp, mask, rows),
        name="gossip_step",
        out_shape=(state, state, state),
        in_specs=[hbm] * 5,
        out_specs=(hbm, hbm, hbm),
        scratch_shapes=[
            pltpu.VMEM((2 * tok, feat), BF16),
            pltpu.VMEM((3, 3, rows, width), F32),
            pltpu.VMEM((3, depth, width), F32),
            pltpu.VMEM((3, depth, width), BF16),
            pltpu.VMEM((3, depth, width), BF16),
            pltpu.VMEM((n_tp, depth, feat), BF16),
            pltpu.VMEM((n_tp, n_tp, depth, tok), F32),
            pltpu.VMEM((n_tp, depth, tok), F32),
            pltpu.VMEM((n_tp, depth, tok), F32),
            pltpu.VMEM((n_tp, depth, feat), BF16),
            pltpu.VMEM((n_tp, depth, feat), BF16),
            pltpu.VMEM((n_tp, depth, feat), BF16),
            pltpu.VMEM((8, LANE), F32),
            pltpu.VMEM((n_tp, 8, LANE), F32),
            pltpu.VMEM((8, LANE), F32),
            pltpu.VMEM((8, LANE), F32),
            pltpu.VMEM((3, depth, width), F32),
            pltpu.VMEM((3, 3, rows, width), F32),
            dma((5,)),
            dma((3,)),
            dma(many), dma(many),
            dma(many), dma(many),
            dma(many), dma(many),
            dma(many), dma(many),
            dma((3,)), dma((3,)),
            dma((n_tp,)), dma((n_tp,)),
            dma((1,)), dma((1,)),
        ],
        compiler_params=pltpu.CompilerParams(
            collective_id=mask, has_side_effects=True, vmem_limit_bytes=32 * 1024 * 1024
        ),
    )(x, dy, w, m, v)


def solution(mesh):
    n_rep = mesh.shape["rep"]
    n_tp = mesh.shape["tp"]

    def per_device(inputs, out_grads, weights, first_moment, second_moment, partners):
        branches = [functools.partial(exchange, n_tp, mask) for mask in range(1, n_rep)]
        return lax.switch(
            partners[0, 0] - 1, branches,
            inputs, out_grads, weights, first_moment, second_moment,
        )

    return jax.shard_map(
        per_device,
        mesh=mesh,
        in_specs=(
            P("rep", None, None, "tp"),
            P("rep", None, None, "tp"),
            P("rep", None, "tp", None),
            P("rep", None, "tp", None),
            P("rep", None, "tp", None),
            P(),
        ),
        out_specs=(
            P("rep", None, "tp", None),
            P("rep", None, "tp", None),
            P("rep", None, "tp", None),
        ),
        check_vma=False,
    )
```

```python
import functools

import jax
import jax.numpy as jnp
from jax import lax
from jax.experimental import pallas as pl
from jax.experimental.pallas import tpu as pltpu
from jax.sharding import PartitionSpec as P

STEP0 = 1000
CLIP = 1.0
BETA1 = 0.9
BETA2 = 0.95
LEARN = 0.001
DECAY = 0.1
EPSILON = 1e-08
COUNT = STEP0 + 1
FIX_ONE = 1.0 - BETA1**COUNT
FIX_TWO = 1.0 - BETA2**COUNT

MESH = pl.DeviceIdType.MESH
BF16 = jnp.bfloat16
F32 = jnp.float32
LANE = 128
VMEM_LIMIT = 60 * 1024 * 1024


def flipped(index, mask):
    out = index
    bit = 1
    while bit <= mask:
        if mask & bit:
            out = out + bit * (1 - 2 * ((index // bit) % 2))
        bit *= 2
    return out


def adamw(params, first, second, grads, scale):
    clipped = grads * scale
    first = BETA1 * first + (1.0 - BETA1) * clipped
    second = BETA2 * second + (1.0 - BETA2) * clipped * clipped
    step = first * (1.0 / FIX_ONE) / (jnp.sqrt(second * (1.0 / FIX_TWO)) + EPSILON)
    params = params - LEARN * (step + DECAY * params)
    return params, first, second


def chunk_of(feat):
    return next(size for size in (512, 256, 128) if feat % size == 0)


def kernel(
    n_tp, mask, rows, width,
    x_ref, dy_ref, w_ref, m_ref, v_ref,
    ow_ref, om_ref, ov_ref,
    xy, state, low, mate, lowall, part, sums, deriv,
    gsend, gall, gmate, sq, sqall, sqsum, sqmate,
    load_sem, store_sem,
    low_send, low_recv, part_send, part_recv, g_send, g_recv, sq_send, sq_recv,
    early_send, early_recv, fwd_send, fwd_recv, sqm_send, sqm_recv,
):
    rep = lax.axis_index("rep")
    tp = lax.axis_index("tp")
    partner = flipped(rep, mask)
    tok = x_ref.shape[2]
    feat = x_ref.shape[3]
    tiles = width // LANE
    depth = low.shape[1]
    used = 3 * rows
    chunk = chunk_of(feat)

    kept = pl.ds(0, used * tiles)
    loads = [
        pltpu.make_async_copy(w_ref, state.at[0, kept], load_sem.at[0]),
        pltpu.make_async_copy(x_ref.at[0, 0], xy.at[pl.ds(0, tok)], load_sem.at[1]),
        pltpu.make_async_copy(dy_ref.at[0, 0], xy.at[pl.ds(tok, tok)], load_sem.at[2]),
        pltpu.make_async_copy(m_ref, state.at[1, kept], load_sem.at[3]),
        pltpu.make_async_copy(v_ref, state.at[2, kept], load_sem.at[4]),
    ]
    for load in loads:
        load.start()

    barrier = pltpu.get_barrier_semaphore()
    peers = [lax.rem(tp + d, n_tp) for d in range(1, n_tp)]
    sources = [lax.rem(tp + n_tp - d, n_tp) for d in range(1, n_tp)]
    for peer in peers:
        pl.semaphore_signal(barrier, inc=1, device_id={"tp": peer}, device_id_type=MESH)
    pl.semaphore_signal(barrier, inc=1, device_id={"rep": partner}, device_id_type=MESH)

    def to_peer(src, dst, send, recv, peer):
        return pltpu.make_async_remote_copy(
            src_ref=src, dst_ref=dst, send_sem=send, recv_sem=recv,
            device_id={"tp": peer}, device_id_type=MESH,
        )

    def to_mate(src, dst, send, recv):
        return pltpu.make_async_remote_copy(
            src_ref=src, dst_ref=dst, send_sem=send, recv_sem=recv,
            device_id={"rep": partner}, device_id_type=MESH,
        )

    def columns(block):
        return pl.ds(pl.multiple_of(block * feat, LANE), feat)

    def lines(j):
        return pl.ds(j, depth, stride=tiles)

    def lanes(j):
        return pl.ds(pl.multiple_of(j * LANE, LANE), LANE)

    if used < depth:
        spare = (depth - used) * tiles
        state[:, pl.ds(used * tiles, spare), :] = jnp.zeros((3, spare, LANE), F32)

    def round_state(which):
        @pl.loop(0, tiles // 4)
        def _(i):
            for u in range(4):
                j = i * 4 + u
                low[which, :, lanes(j)] = state[which, lines(j), :].astype(BF16)

    loads[0].wait()
    round_state(0)
    pl.semaphore_wait(barrier, n_tp)
    low_copies = [
        to_peer(low.at[0, :, columns(peer)], lowall.at[tp], low_send.at[d], low_recv.at[d], peer)
        for d, peer in enumerate(peers)
    ]
    for copy in low_copies:
        copy.start()
    early = [to_mate(low.at[k], mate.at[k], early_send.at[k], early_recv.at[k]) for k in range(3)]
    early[0].start()
    lowall[tp] = low[0, :, columns(tp)]
    loads[3].wait()
    round_state(1)
    early[1].start()
    loads[4].wait()
    round_state(2)
    early[2].start()

    loads[1].wait()
    loads[2].wait()
    for copy in low_copies:
        copy.wait_recv()

    def piece(i):
        return pl.ds(pl.multiple_of(i * chunk, LANE), chunk)

    def contract(i, acc):
        return acc + lax.dot_general(
            lowall[:, :, piece(i)].reshape(n_tp * depth, chunk), xy[:, piece(i)],
            (((1,), (1,)), ((), ())), preferred_element_type=F32,
        )

    prod = lax.fori_loop(
        0, feat // chunk, contract, jnp.zeros((n_tp * depth, 2 * tok), F32)
    ).reshape(n_tp, depth, 2 * tok)
    row = lax.broadcasted_iota(jnp.int32, (n_tp, depth, tok), 1)
    part[tp] = jnp.where(row < 2 * rows, prod[:, :, :tok], prod[:, :, tok:])
    part_copies = [
        to_peer(part.at[tp], part.at[tp], part_send.at[d], part_recv.at[d], peer)
        for d, peer in enumerate(peers)
    ]
    for copy in part_copies:
        copy.start()
    for copy in part_copies:
        copy.wait_recv()
    total = part[0]
    for t in range(1, n_tp):
        total = total + part[t]
    sums[...] = total
    gate = sums[:, pl.ds(0, rows), :]
    upper = sums[:, pl.ds(rows, rows), :]
    back = sums[:, pl.ds(2 * rows, rows), :]
    sig = jax.nn.sigmoid(gate)
    hidden = (gate * sig * upper).astype(BF16).astype(F32)
    d_up = (back * gate * sig).astype(BF16).astype(F32)
    d_gate = (back * upper * sig * (1.0 + gate * (1.0 - sig))).astype(BF16).astype(F32)
    deriv[:, pl.ds(0, rows), :] = d_gate
    deriv[:, pl.ds(rows, rows), :] = d_up
    deriv[:, pl.ds(2 * rows, rows), :] = hidden
    if used < depth:
        deriv[:, pl.ds(used, depth - used), :] = jnp.zeros((n_tp, depth - used, tok), F32)
    both = deriv[...]
    left = jnp.concatenate(
        [jnp.where(row < 2 * rows, both, 0.0), jnp.where(row < 2 * rows, 0.0, both)], axis=2
    ).astype(BF16).reshape(n_tp * depth, 2 * tok)

    def expand(i, acc):
        grads = jnp.dot(left, xy[:, piece(i)], preferred_element_type=F32)
        gsend[:, :, piece(i)] = grads.astype(BF16).reshape(n_tp, depth, chunk)
        for u in range(chunk // LANE):
            tile = grads[:, u * LANE:(u + 1) * LANE]
            acc = acc + tile * tile
        return acc

    squares = lax.fori_loop(0, feat // chunk, expand, jnp.zeros((n_tp * depth, LANE), F32))
    g_copies = [
        to_peer(gsend.at[peer], gall.at[:, columns(tp)], g_send.at[d], g_recv.at[d], peer)
        for d, peer in enumerate(peers)
    ]
    for copy in g_copies:
        copy.start()
    own = to_mate(gsend.at[tp], gmate.at[:, columns(tp)], fwd_send.at[n_tp - 1], fwd_recv.at[n_tp - 1])
    own.start()
    sq[...] = jnp.broadcast_to(jnp.sum(squares, keepdims=True), sq.shape)
    sqall[tp] = sq[...]
    sq_copies = [
        to_peer(sq, sqall.at[tp], sq_send.at[d], sq_recv.at[d], peer)
        for d, peer in enumerate(peers)
    ]
    for copy in sq_copies:
        copy.start()
    gall[:, columns(tp)] = gsend[tp]

    forwards = []
    for d, source in enumerate(sources):
        g_copies[d].wait_recv()
        half = columns(source)
        copy = to_mate(gall.at[:, half], gmate.at[:, half], fwd_send.at[d], fwd_recv.at[d])
        copy.start()
        forwards.append(copy)
    for copy in sq_copies:
        copy.wait_recv()
    square = sqall[0]
    for t in range(1, n_tp):
        square = square + sqall[t]
    sqsum[...] = square
    sq_mate = to_mate(sqsum, sqmate, sqm_send.at[0], sqm_recv.at[0])
    sq_mate.start()

    def factor_of(square):
        scale = CLIP / jnp.maximum(jnp.sqrt(square), CLIP)
        return jnp.concatenate([scale] * (depth // 8), axis=0)

    factor = factor_of(square)

    @pl.loop(0, tiles // 4)
    def _(i):
        for u in range(4):
            j = i * 4 + u
            new = adamw(
                *(state[k, lines(j), :] for k in range(3)), gall[:, lanes(j)].astype(F32), factor
            )
            for k in range(3):
                state[k, lines(j), :] = new[k]

    for copy in early:
        copy.wait_recv()
    sq_mate.wait_recv()
    own.wait_recv()
    mate_factor = factor_of(sqmate[...])

    def average(j):
        new = adamw(
            *(mate[k, :, lanes(j)].astype(F32) for k in range(3)),
            gmate[:, lanes(j)].astype(F32), mate_factor,
        )
        for k in range(3):
            state[k, lines(j), :] = 0.5 * (state[k, lines(j), :] + new[k])

    share = tiles // n_tp

    @pl.loop(0, share // 5)
    def _(i):
        for u in range(5):
            average(tp * share + i * 5 + u)

    for copy in forwards:
        copy.wait_recv()

    @pl.loop(0, (tiles - share) // 5)
    def _(i):
        for u in range(5):
            average(lax.rem((tp + 1) * share + i * 5 + u, tiles))

    stores = []
    for which, ref in enumerate((ow_ref, om_ref, ov_ref)):
        store = pltpu.make_async_copy(state.at[which, kept], ref, store_sem.at[which])
        store.start()
        stores.append(store)
    for copy in low_copies + part_copies + g_copies + sq_copies + early + forwards + [own, sq_mate]:
        copy.wait_send()
    for store in stores:
        store.wait()


def exchange(n_tp, mask, x, dy, w, m, v):
    _, _, tok, feat = x.shape
    shape = w.shape
    _, _, rows, width = shape
    depth = -(-3 * rows // 16) * 16
    tiles = width // LANE
    dma = pltpu.SemaphoreType.DMA
    hbm = pl.BlockSpec(memory_space=pl.ANY)
    many = (max(n_tp - 1, 1),)
    flat = (3 * rows * tiles, LANE)
    out = jax.ShapeDtypeStruct(flat, F32)
    new = pl.pallas_call(
        functools.partial(kernel, n_tp, mask, rows, width),
        name="gossip_step",
        out_shape=(out, out, out),
        in_specs=[hbm] * 5,
        out_specs=(hbm, hbm, hbm),
        scratch_shapes=[
            pltpu.VMEM((2 * tok, feat), BF16),
            pltpu.VMEM((3, depth * tiles, LANE), F32),
            pltpu.VMEM((3, depth, width), BF16),
            pltpu.VMEM((3, depth, width), BF16),
            pltpu.VMEM((n_tp, depth, feat), BF16),
            pltpu.VMEM((n_tp, n_tp, depth, tok), F32),
            pltpu.VMEM((n_tp, depth, tok), F32),
            pltpu.VMEM((n_tp, depth, tok), F32),
            pltpu.VMEM((n_tp, depth, feat), BF16),
            pltpu.VMEM((depth, width), BF16),
            pltpu.VMEM((depth, width), BF16),
            pltpu.VMEM((8, LANE), F32),
            pltpu.VMEM((n_tp, 8, LANE), F32),
            pltpu.VMEM((8, LANE), F32),
            pltpu.VMEM((8, LANE), F32),
            dma((5,)),
            dma((3,)),
            dma(many), dma(many),
            dma(many), dma(many),
            dma(many), dma(many),
            dma(many), dma(many),
            dma((3,)), dma((3,)),
            dma((n_tp,)), dma((n_tp,)),
            dma((1,)), dma((1,)),
        ],
        compiler_params=pltpu.CompilerParams(
            collective_id=mask, has_side_effects=True, vmem_limit_bytes=VMEM_LIMIT
        ),
    )(x, dy, *(value.reshape(flat) for value in (w, m, v)))
    return tuple(value.reshape(shape) for value in new)


def solution(mesh):
    n_rep = mesh.shape["rep"]
    n_tp = mesh.shape["tp"]

    def per_device(inputs, out_grads, weights, first_moment, second_moment, partners):
        branches = [functools.partial(exchange, n_tp, mask) for mask in range(1, n_rep)]
        return lax.switch(
            partners[0, 0] - 1, branches,
            inputs, out_grads, weights, first_moment, second_moment,
        )

    return jax.shard_map(
        per_device,
        mesh=mesh,
        in_specs=(
            P("rep", None, None, "tp"),
            P("rep", None, None, "tp"),
            P("rep", None, "tp", None),
            P("rep", None, "tp", None),
            P("rep", None, "tp", None),
            P(),
        ),
        out_specs=(
            P("rep", None, "tp", None),
            P("rep", None, "tp", None),
            P("rep", None, "tp", None),
        ),
        check_vma=False,
    )
```

```python
import functools

import jax
import jax.numpy as jnp
from jax import lax
from jax.experimental import pallas as pl
from jax.experimental.pallas import tpu as pltpu
from jax.sharding import PartitionSpec as P

STEP0 = 1000
CLIP = 1.0
BETA1 = 0.9
BETA2 = 0.95
LEARN = 0.001
DECAY = 0.1
EPSILON = 1e-08
COUNT = STEP0 + 1
FIX_ONE = 1.0 - BETA1**COUNT
FIX_TWO = 1.0 - BETA2**COUNT

MESH = pl.DeviceIdType.MESH
BF16 = jnp.bfloat16
F32 = jnp.float32
LANE = 128
FAR = 8
VMEM_LIMIT = 60 * 1024 * 1024


def flipped(index, mask):
    out = index
    bit = 1
    while bit <= mask:
        if mask & bit:
            out = out + bit * (1 - 2 * ((index // bit) % 2))
        bit *= 2
    return out


def adamw(params, first, second, grads, scale):
    clipped = grads * scale
    first = BETA1 * first + (1.0 - BETA1) * clipped
    second = BETA2 * second + (1.0 - BETA2) * clipped * clipped
    step = first * (1.0 / FIX_ONE) / (jnp.sqrt(second * (1.0 / FIX_TWO)) + EPSILON)
    params = params - LEARN * (step + DECAY * params)
    return params, first, second


def chunk_of(feat):
    return next(size for size in (512, 256, 128) if feat % size == 0)


def kernel(
    n_tp, mask, rows, width,
    x_ref, dy_ref, w_ref, m_ref, v_ref,
    ow_ref, om_ref, ov_ref,
    xy, state, low, mate, lowall, part, sums, deriv,
    gsend, gall, gmate, sq, sqall, sqsum, sqmate,
    load_sem, store_sem,
    low_send, low_recv, part_send, part_recv, g_send, g_recv, sq_send, sq_recv,
    early_send, early_recv, fwd_send, fwd_recv, sqm_send, sqm_recv, late_send, late_recv,
):
    far = mask >= FAR
    rep = lax.axis_index("rep")
    tp = lax.axis_index("tp")
    partner = flipped(rep, mask)
    tok = x_ref.shape[2]
    feat = x_ref.shape[3]
    tiles = width // LANE
    depth = low.shape[1]
    used = 3 * rows
    chunk = chunk_of(feat)

    kept = pl.ds(0, used * tiles)
    loads = [
        pltpu.make_async_copy(w_ref, state.at[0, kept], load_sem.at[0]),
        pltpu.make_async_copy(x_ref.at[0, 0], xy.at[pl.ds(0, tok)], load_sem.at[1]),
        pltpu.make_async_copy(dy_ref.at[0, 0], xy.at[pl.ds(tok, tok)], load_sem.at[2]),
        pltpu.make_async_copy(m_ref, state.at[1, kept], load_sem.at[3]),
        pltpu.make_async_copy(v_ref, state.at[2, kept], load_sem.at[4]),
    ]
    for load in loads:
        load.start()

    barrier = pltpu.get_barrier_semaphore()
    peers = [lax.rem(tp + d, n_tp) for d in range(1, n_tp)]
    sources = [lax.rem(tp + n_tp - d, n_tp) for d in range(1, n_tp)]
    for peer in peers:
        pl.semaphore_signal(barrier, inc=1, device_id={"tp": peer}, device_id_type=MESH)
    pl.semaphore_signal(barrier, inc=1, device_id={"rep": partner}, device_id_type=MESH)

    def to_peer(src, dst, send, recv, peer):
        return pltpu.make_async_remote_copy(
            src_ref=src, dst_ref=dst, send_sem=send, recv_sem=recv,
            device_id={"tp": peer}, device_id_type=MESH,
        )

    def to_mate(src, dst, send, recv):
        return pltpu.make_async_remote_copy(
            src_ref=src, dst_ref=dst, send_sem=send, recv_sem=recv,
            device_id={"rep": partner}, device_id_type=MESH,
        )

    def columns(block):
        return pl.ds(pl.multiple_of(block * feat, LANE), feat)

    def lines(j):
        return pl.ds(j, depth, stride=tiles)

    def lanes(j):
        return pl.ds(pl.multiple_of(j * LANE, LANE), LANE)

    if used < depth:
        spare = (depth - used) * tiles
        state[:, pl.ds(used * tiles, spare), :] = jnp.zeros((3, spare, LANE), F32)

    def round_state(which):
        @pl.loop(0, tiles // 4)
        def _(i):
            for u in range(4):
                j = i * 4 + u
                low[which, :, lanes(j)] = state[which, lines(j), :].astype(BF16)

    loads[0].wait()
    round_state(0)
    pl.semaphore_wait(barrier, n_tp)
    low_copies = [
        to_peer(low.at[0, :, columns(peer)], lowall.at[tp], low_send.at[d], low_recv.at[d], peer)
        for d, peer in enumerate(peers)
    ]
    for copy in low_copies:
        copy.start()
    span = columns(tp) if far else pl.ds(0, width)
    early = [
        to_mate(low.at[k, :, span], mate.at[k, :, span], early_send.at[k], early_recv.at[k])
        for k in range(3)
    ]
    early[0].start()
    lowall[tp] = low[0, :, columns(tp)]
    loads[3].wait()
    round_state(1)
    early[1].start()
    loads[4].wait()
    round_state(2)
    early[2].start()

    loads[1].wait()
    loads[2].wait()
    for copy in low_copies:
        copy.wait_recv()

    def piece(i):
        return pl.ds(pl.multiple_of(i * chunk, LANE), chunk)

    def contract(i, acc):
        return acc + lax.dot_general(
            lowall[:, :, piece(i)].reshape(n_tp * depth, chunk), xy[:, piece(i)],
            (((1,), (1,)), ((), ())), preferred_element_type=F32,
        )

    prod = lax.fori_loop(
        0, feat // chunk, contract, jnp.zeros((n_tp * depth, 2 * tok), F32)
    ).reshape(n_tp, depth, 2 * tok)
    row = lax.broadcasted_iota(jnp.int32, (n_tp, depth, tok), 1)
    part[tp] = jnp.where(row < 2 * rows, prod[:, :, :tok], prod[:, :, tok:])
    part_copies = [
        to_peer(part.at[tp], part.at[tp], part_send.at[d], part_recv.at[d], peer)
        for d, peer in enumerate(peers)
    ]
    for copy in part_copies:
        copy.start()
    for copy in part_copies:
        copy.wait_recv()
    total = part[0]
    for t in range(1, n_tp):
        total = total + part[t]
    sums[...] = total
    gate = sums[:, pl.ds(0, rows), :]
    upper = sums[:, pl.ds(rows, rows), :]
    back = sums[:, pl.ds(2 * rows, rows), :]
    sig = jax.nn.sigmoid(gate)
    hidden = (gate * sig * upper).astype(BF16).astype(F32)
    d_up = (back * gate * sig).astype(BF16).astype(F32)
    d_gate = (back * upper * sig * (1.0 + gate * (1.0 - sig))).astype(BF16).astype(F32)
    deriv[:, pl.ds(0, rows), :] = d_gate
    deriv[:, pl.ds(rows, rows), :] = d_up
    deriv[:, pl.ds(2 * rows, rows), :] = hidden
    if used < depth:
        deriv[:, pl.ds(used, depth - used), :] = jnp.zeros((n_tp, depth - used, tok), F32)
    both = deriv[...]
    left = jnp.concatenate(
        [jnp.where(row < 2 * rows, both, 0.0), jnp.where(row < 2 * rows, 0.0, both)], axis=2
    ).astype(BF16).reshape(n_tp * depth, 2 * tok)

    def expand(i, acc):
        grads = jnp.dot(left, xy[:, piece(i)], preferred_element_type=F32)
        gsend[:, :, piece(i)] = grads.astype(BF16).reshape(n_tp, depth, chunk)
        for u in range(chunk // LANE):
            tile = grads[:, u * LANE:(u + 1) * LANE]
            acc = acc + tile * tile
        return acc

    squares = lax.fori_loop(0, feat // chunk, expand, jnp.zeros((n_tp * depth, LANE), F32))
    g_copies = [
        to_peer(gsend.at[peer], gall.at[:, columns(tp)], g_send.at[d], g_recv.at[d], peer)
        for d, peer in enumerate(peers)
    ]
    for copy in g_copies:
        copy.start()
    own = to_mate(gsend.at[tp], gmate.at[:, columns(tp)], fwd_send.at[n_tp - 1], fwd_recv.at[n_tp - 1])
    own.start()
    sq[...] = jnp.broadcast_to(jnp.sum(squares, keepdims=True), sq.shape)
    sqall[tp] = sq[...]
    sq_copies = [
        to_peer(sq, sqall.at[tp], sq_send.at[d], sq_recv.at[d], peer)
        for d, peer in enumerate(peers)
    ]
    for copy in sq_copies:
        copy.start()
    gall[:, columns(tp)] = gsend[tp]

    forwards = []
    for d, source in enumerate(sources):
        g_copies[d].wait_recv()
        if not far:
            half = columns(source)
            copy = to_mate(gall.at[:, half], gmate.at[:, half], fwd_send.at[d], fwd_recv.at[d])
            copy.start()
            forwards.append(copy)
    for copy in sq_copies:
        copy.wait_recv()
    square = sqall[0]
    for t in range(1, n_tp):
        square = square + sqall[t]
    sqsum[...] = square
    sq_mate = to_mate(sqsum, sqmate, sqm_send.at[0], sqm_recv.at[0])
    sq_mate.start()

    def factor_of(square):
        scale = CLIP / jnp.maximum(jnp.sqrt(square), CLIP)
        return jnp.concatenate([scale] * (depth // 8), axis=0)

    factor = factor_of(square)
    share = tiles // n_tp

    def own_columns(body):
        @pl.loop(0, share // 5)
        def _(i):
            for u in range(5):
                body(tp * share + i * 5 + u)

    def other_columns(body):
        @pl.loop(0, (tiles - share) // 5)
        def _(i):
            for u in range(5):
                body(lax.rem((tp + 1) * share + i * 5 + u, tiles))

    def update(j, keep=False):
        new = adamw(
            *(state[k, lines(j), :] for k in range(3)), gall[:, lanes(j)].astype(F32), factor
        )
        for k in range(3):
            state[k, lines(j), :] = new[k]
            if keep:
                low[k, :, lanes(j)] = new[k].astype(BF16)

    def average(j):
        new = adamw(
            *(mate[k, :, lanes(j)].astype(F32) for k in range(3)),
            gmate[:, lanes(j)].astype(F32), mate_factor,
        )
        for k in range(3):
            state[k, lines(j), :] = 0.5 * (state[k, lines(j), :] + new[k])

    late = []
    if far:
        for copy in low_copies:
            copy.wait_send()
        other_columns(functools.partial(update, keep=True))
        for k in range(3):
            late.append([
                to_mate(
                    low.at[k, :, columns(source)], mate.at[k, :, columns(source)],
                    late_send.at[k, d], late_recv.at[k, d],
                )
                for d, source in enumerate(sources)
            ])
            for copy in late[k]:
                copy.start()
    else:
        other_columns(update)
    own_columns(update)

    for copy in early:
        copy.wait_recv()
    sq_mate.wait_recv()
    own.wait_recv()
    mate_factor = factor_of(sqmate[...])
    own_columns(average)

    outs = (ow_ref, om_ref, ov_ref)
    stores = [
        pltpu.make_async_copy(state.at[k, kept], outs[k], store_sem.at[k]) for k in range(3)
    ]
    if far:
        for k in range(3):
            for copy in late[k]:
                copy.wait_recv()

            def blend(j):
                state[k, lines(j), :] = 0.5 * (
                    state[k, lines(j), :] + mate[k, :, lanes(j)].astype(F32)
                )

            other_columns(blend)
            stores[k].start()
    else:
        for copy in forwards:
            copy.wait_recv()
        other_columns(average)
        for store in stores:
            store.start()
    if not far:
        for copy in low_copies:
            copy.wait_send()
    for copies in late:
        for copy in copies:
            copy.wait_send()
    for copy in part_copies + g_copies + sq_copies + early + forwards + [own, sq_mate]:
        copy.wait_send()
    for store in stores:
        store.wait()


def exchange(n_tp, mask, x, dy, w, m, v):
    _, _, tok, feat = x.shape
    shape = w.shape
    _, _, rows, width = shape
    depth = -(-3 * rows // 16) * 16
    tiles = width // LANE
    dma = pltpu.SemaphoreType.DMA
    hbm = pl.BlockSpec(memory_space=pl.ANY)
    many = (max(n_tp - 1, 1),)
    flat = (3 * rows * tiles, LANE)
    out = jax.ShapeDtypeStruct(flat, F32)
    new = pl.pallas_call(
        functools.partial(kernel, n_tp, mask, rows, width),
        name="gossip_step",
        out_shape=(out, out, out),
        in_specs=[hbm] * 5,
        out_specs=(hbm, hbm, hbm),
        scratch_shapes=[
            pltpu.VMEM((2 * tok, feat), BF16),
            pltpu.VMEM((3, depth * tiles, LANE), F32),
            pltpu.VMEM((3, depth, width), BF16),
            pltpu.VMEM((3, depth, width), BF16),
            pltpu.VMEM((n_tp, depth, feat), BF16),
            pltpu.VMEM((n_tp, n_tp, depth, tok), F32),
            pltpu.VMEM((n_tp, depth, tok), F32),
            pltpu.VMEM((n_tp, depth, tok), F32),
            pltpu.VMEM((n_tp, depth, feat), BF16),
            pltpu.VMEM((depth, width), BF16),
            pltpu.VMEM((depth, width), BF16),
            pltpu.VMEM((8, LANE), F32),
            pltpu.VMEM((n_tp, 8, LANE), F32),
            pltpu.VMEM((8, LANE), F32),
            pltpu.VMEM((8, LANE), F32),
            dma((5,)),
            dma((3,)),
            dma(many), dma(many),
            dma(many), dma(many),
            dma(many), dma(many),
            dma(many), dma(many),
            dma((3,)), dma((3,)),
            dma((n_tp,)), dma((n_tp,)),
            dma((1,)), dma((1,)),
            dma((3,) + many), dma((3,) + many),
        ],
        compiler_params=pltpu.CompilerParams(
            collective_id=mask, has_side_effects=True, vmem_limit_bytes=VMEM_LIMIT
        ),
    )(x, dy, *(value.reshape(flat) for value in (w, m, v)))
    return new


def place(*refs):
    copies = [
        pltpu.make_async_copy(refs[k], refs[3 + k], refs[6].at[k]) for k in range(3)
    ]
    for copy in copies:
        copy.start()
    for copy in copies:
        copy.wait()


def placed(arrays):
    hbm = pl.BlockSpec(memory_space=pl.ANY)
    return pl.pallas_call(
        place,
        name="place",
        out_shape=tuple(jax.ShapeDtypeStruct(value.shape, value.dtype) for value in arrays),
        in_specs=[hbm] * 3,
        out_specs=(hbm,) * 3,
        scratch_shapes=[pltpu.SemaphoreType.DMA((3,))],
    )(*arrays)


def solution(mesh):
    n_rep = mesh.shape["rep"]
    n_tp = mesh.shape["tp"]

    def per_device(inputs, out_grads, weights, first_moment, second_moment, partners):
        branches = [functools.partial(exchange, n_tp, mask) for mask in range(1, n_rep)]
        new = lax.switch(
            partners[0, 0] - 1, branches,
            inputs, out_grads, weights, first_moment, second_moment,
        )
        return tuple(value.reshape(weights.shape) for value in placed(new))

    return jax.shard_map(
        per_device,
        mesh=mesh,
        in_specs=(
            P("rep", None, None, "tp"),
            P("rep", None, None, "tp"),
            P("rep", None, "tp", None),
            P("rep", None, "tp", None),
            P("rep", None, "tp", None),
            P(),
        ),
        out_specs=(
            P("rep", None, "tp", None),
            P("rep", None, "tp", None),
            P("rep", None, "tp", None),
        ),
        check_vma=False,
    )
```

```python
import functools

import jax
import jax.numpy as jnp
from jax import lax
from jax.experimental import pallas as pl
from jax.experimental.pallas import tpu as pltpu
from jax.sharding import PartitionSpec as P

STEP0 = 1000
CLIP = 1.0
BETA1 = 0.9
BETA2 = 0.95
LEARN = 0.001
DECAY = 0.1
EPSILON = 1e-08
COUNT = STEP0 + 1
FIX_ONE = 1.0 - BETA1**COUNT
FIX_TWO = 1.0 - BETA2**COUNT

MESH = pl.DeviceIdType.MESH
BF16 = jnp.bfloat16
F32 = jnp.float32
LANE = 128
FAR = 8
VMEM_LIMIT = 60 * 1024 * 1024


def flipped(index, mask):
    out = index
    bit = 1
    while bit <= mask:
        if mask & bit:
            out = out + bit * (1 - 2 * ((index // bit) % 2))
        bit *= 2
    return out


def adamw(params, first, second, grads, scale):
    clipped = grads * scale
    first = BETA1 * first + (1.0 - BETA1) * clipped
    second = BETA2 * second + (1.0 - BETA2) * clipped * clipped
    step = first * (1.0 / FIX_ONE) / (jnp.sqrt(second * (1.0 / FIX_TWO)) + EPSILON)
    params = params - LEARN * (step + DECAY * params)
    return params, first, second


def chunk_of(feat):
    return next(size for size in (512, 256, 128) if feat % size == 0)


def kernel(
    n_tp, mask, rows, width,
    x_ref, dy_ref, w_ref, m_ref, v_ref,
    ow_ref, om_ref, ov_ref,
    xy, state, low, mate, lowall, part, sums, deriv,
    gsend, gall, gmate, sq, sqall, sqsum, sqmate,
    load_sem, store_sem,
    low_send, low_recv, part_send, part_recv, g_send, g_recv, sq_send, sq_recv,
    early_send, early_recv, fwd_send, fwd_recv, sqm_send, sqm_recv, late_send, late_recv,
):
    far = mask >= FAR
    rep = lax.axis_index("rep")
    tp = lax.axis_index("tp")
    partner = flipped(rep, mask)
    tok = x_ref.shape[2]
    feat = x_ref.shape[3]
    tiles = width // LANE
    share = tiles // n_tp
    ahead = share * 15 // 20 if far and share % 20 == 0 else share
    unroll = 5 if ahead % 5 == 0 else 4
    depth = low.shape[1]
    used = 3 * rows
    chunk = chunk_of(feat)

    kept = pl.ds(0, used * tiles)
    loads = [
        pltpu.make_async_copy(w_ref, state.at[0, kept], load_sem.at[0]),
        pltpu.make_async_copy(x_ref.at[0, 0], xy.at[pl.ds(0, tok)], load_sem.at[1]),
        pltpu.make_async_copy(dy_ref.at[0, 0], xy.at[pl.ds(tok, tok)], load_sem.at[2]),
        pltpu.make_async_copy(m_ref, state.at[1, kept], load_sem.at[3]),
        pltpu.make_async_copy(v_ref, state.at[2, kept], load_sem.at[4]),
    ]
    for load in loads:
        load.start()

    barrier = pltpu.get_barrier_semaphore()
    peers = [lax.rem(tp + d, n_tp) for d in range(1, n_tp)]
    sources = [lax.rem(tp + n_tp - d, n_tp) for d in range(1, n_tp)]
    for peer in peers:
        pl.semaphore_signal(barrier, inc=1, device_id={"tp": peer}, device_id_type=MESH)
    pl.semaphore_signal(barrier, inc=1, device_id={"rep": partner}, device_id_type=MESH)

    def to_peer(src, dst, send, recv, peer):
        return pltpu.make_async_remote_copy(
            src_ref=src, dst_ref=dst, send_sem=send, recv_sem=recv,
            device_id={"tp": peer}, device_id_type=MESH,
        )

    def to_mate(src, dst, send, recv):
        return pltpu.make_async_remote_copy(
            src_ref=src, dst_ref=dst, send_sem=send, recv_sem=recv,
            device_id={"rep": partner}, device_id_type=MESH,
        )

    def columns(block):
        return pl.ds(pl.multiple_of(block * feat, LANE), feat)

    def lines(j):
        return pl.ds(j, depth, stride=tiles)

    def lanes(j):
        return pl.ds(pl.multiple_of(j * LANE, LANE), LANE)

    if used < depth:
        spare = (depth - used) * tiles
        state[:, pl.ds(used * tiles, spare), :] = jnp.zeros((3, spare, LANE), F32)

    def round_state(which):
        @pl.loop(0, tiles // 4)
        def _(i):
            for u in range(4):
                j = i * 4 + u
                low[which, :, lanes(j)] = state[which, lines(j), :].astype(BF16)

    loads[0].wait()
    round_state(0)
    pl.semaphore_wait(barrier, n_tp)
    low_copies = [
        to_peer(low.at[0, :, columns(peer)], lowall.at[tp], low_send.at[d], low_recv.at[d], peer)
        for d, peer in enumerate(peers)
    ]
    for copy in low_copies:
        copy.start()
    def front(block):
        return pl.ds(pl.multiple_of(block * feat, LANE), ahead * LANE)

    span = front(tp) if far else pl.ds(0, width)
    early = [
        to_mate(low.at[k, :, span], mate.at[k, :, span], early_send.at[k], early_recv.at[k])
        for k in range(3)
    ]
    early[0].start()
    lowall[tp] = low[0, :, columns(tp)]
    loads[3].wait()
    round_state(1)
    early[1].start()
    loads[4].wait()
    round_state(2)
    early[2].start()

    loads[1].wait()
    loads[2].wait()
    for copy in low_copies:
        copy.wait_recv()

    def piece(i):
        return pl.ds(pl.multiple_of(i * chunk, LANE), chunk)

    def contract(i, acc):
        return acc + lax.dot_general(
            lowall[:, :, piece(i)].reshape(n_tp * depth, chunk), xy[:, piece(i)],
            (((1,), (1,)), ((), ())), preferred_element_type=F32,
        )

    prod = lax.fori_loop(
        0, feat // chunk, contract, jnp.zeros((n_tp * depth, 2 * tok), F32)
    ).reshape(n_tp, depth, 2 * tok)
    row = lax.broadcasted_iota(jnp.int32, (n_tp, depth, tok), 1)
    part[tp] = jnp.where(row < 2 * rows, prod[:, :, :tok], prod[:, :, tok:])
    part_copies = [
        to_peer(part.at[tp], part.at[tp], part_send.at[d], part_recv.at[d], peer)
        for d, peer in enumerate(peers)
    ]
    for copy in part_copies:
        copy.start()
    for copy in part_copies:
        copy.wait_recv()
    total = part[0]
    for t in range(1, n_tp):
        total = total + part[t]
    sums[...] = total
    gate = sums[:, pl.ds(0, rows), :]
    upper = sums[:, pl.ds(rows, rows), :]
    back = sums[:, pl.ds(2 * rows, rows), :]
    sig = jax.nn.sigmoid(gate)
    hidden = (gate * sig * upper).astype(BF16).astype(F32)
    d_up = (back * gate * sig).astype(BF16).astype(F32)
    d_gate = (back * upper * sig * (1.0 + gate * (1.0 - sig))).astype(BF16).astype(F32)
    deriv[:, pl.ds(0, rows), :] = d_gate
    deriv[:, pl.ds(rows, rows), :] = d_up
    deriv[:, pl.ds(2 * rows, rows), :] = hidden
    if used < depth:
        deriv[:, pl.ds(used, depth - used), :] = jnp.zeros((n_tp, depth - used, tok), F32)
    both = deriv[...]
    left = jnp.concatenate(
        [jnp.where(row < 2 * rows, both, 0.0), jnp.where(row < 2 * rows, 0.0, both)], axis=2
    ).astype(BF16).reshape(n_tp * depth, 2 * tok)

    def expand(i, acc):
        grads = jnp.dot(left, xy[:, piece(i)], preferred_element_type=F32)
        gsend[:, :, piece(i)] = grads.astype(BF16).reshape(n_tp, depth, chunk)
        for u in range(chunk // LANE):
            tile = grads[:, u * LANE:(u + 1) * LANE]
            acc = acc + tile * tile
        return acc

    squares = lax.fori_loop(0, feat // chunk, expand, jnp.zeros((n_tp * depth, LANE), F32))
    sq[...] = jnp.broadcast_to(jnp.sum(squares, keepdims=True), sq.shape)
    sqall[tp] = sq[...]
    sq_copies = [
        to_peer(sq, sqall.at[tp], sq_send.at[d], sq_recv.at[d], peer)
        for d, peer in enumerate(peers)
    ]
    for copy in sq_copies:
        copy.start()
    g_copies = [
        to_peer(gsend.at[peer], gall.at[:, columns(tp)], g_send.at[d], g_recv.at[d], peer)
        for d, peer in enumerate(peers)
    ]
    for copy in g_copies:
        copy.start()
    own = to_mate(
        gsend.at[tp, :, pl.ds(0, ahead * LANE)], gmate.at[:, front(tp)],
        fwd_send.at[n_tp - 1], fwd_recv.at[n_tp - 1],
    )
    own.start()
    gall[:, columns(tp)] = gsend[tp]

    for copy in sq_copies:
        copy.wait_recv()
    square = sqall[0]
    for t in range(1, n_tp):
        square = square + sqall[t]
    sqsum[...] = square
    sq_mate = to_mate(sqsum, sqmate, sqm_send.at[0], sqm_recv.at[0])
    sq_mate.start()

    def factor_of(square):
        scale = CLIP / jnp.maximum(jnp.sqrt(square), CLIP)
        return jnp.concatenate([scale] * (depth // 8), axis=0)

    factor = factor_of(square)

    def own_columns(body):
        @pl.loop(0, ahead // unroll)
        def _(i):
            for u in range(unroll):
                body(tp * share + i * unroll + u)

    def rest_columns(body):
        @pl.loop(0, (share - ahead) // unroll)
        def _(i):
            for u in range(unroll):
                body(tp * share + ahead + i * unroll + u)

    def other_columns(body):
        @pl.loop(0, (tiles - share) // unroll)
        def _(i):
            for u in range(unroll):
                body(lax.rem((tp + 1) * share + i * unroll + u, tiles))

    def update(j, keep=False):
        new = adamw(
            *(state[k, lines(j), :] for k in range(3)), gall[:, lanes(j)].astype(F32), factor
        )
        for k in range(3):
            state[k, lines(j), :] = new[k]
            if keep:
                low[k, :, lanes(j)] = new[k].astype(BF16)

    def average(j):
        new = adamw(
            *(mate[k, :, lanes(j)].astype(F32) for k in range(3)),
            gmate[:, lanes(j)].astype(F32), mate_factor,
        )
        for k in range(3):
            state[k, lines(j), :] = 0.5 * (state[k, lines(j), :] + new[k])

    late = []

    def send_late(cols, at):
        copies = [
            to_mate(low.at[k, :, cols], mate.at[k, :, cols], late_send.at[k, at], late_recv.at[k, at])
            for k in range(3)
        ]
        for copy in copies:
            copy.start()
        late.append(copies)

    if far:
        for copy in low_copies:
            copy.wait_send()
        if ahead < share:
            rest_columns(functools.partial(update, keep=True))
            begin = pl.multiple_of(tp * feat + ahead * LANE, LANE)
            send_late(pl.ds(begin, (share - ahead) * LANE), n_tp - 1)
    forwards = []
    for d, source in enumerate(sources):
        g_copies[d].wait_recv()
        if not far:
            half = columns(source)
            copy = to_mate(gall.at[:, half], gmate.at[:, half], fwd_send.at[d], fwd_recv.at[d])
            copy.start()
            forwards.append(copy)
    if far:
        other_columns(functools.partial(update, keep=True))
        for d, source in enumerate(sources):
            send_late(columns(source), d)
    else:
        other_columns(update)
    own_columns(update)

    for copy in early:
        copy.wait_recv()
    sq_mate.wait_recv()
    own.wait_recv()
    mate_factor = factor_of(sqmate[...])
    own_columns(average)

    outs = (ow_ref, om_ref, ov_ref)
    stores = [
        pltpu.make_async_copy(state.at[k, kept], outs[k], store_sem.at[k]) for k in range(3)
    ]
    def blend(k, j):
        state[k, lines(j), :] = 0.5 * (state[k, lines(j), :] + mate[k, :, lanes(j)].astype(F32))

    if far:
        if ahead < share:
            for k in range(3):
                late[0][k].wait_recv()

            def blend_all(j):
                for k in range(3):
                    blend(k, j)

            rest_columns(blend_all)
        for k in range(3):
            for copies in late[1 if ahead < share else 0:]:
                copies[k].wait_recv()
            other_columns(functools.partial(blend, k))
            stores[k].start()
    else:
        for copy in forwards:
            copy.wait_recv()
        other_columns(average)
        for store in stores:
            store.start()
    if not far:
        for copy in low_copies:
            copy.wait_send()
    for copies in late:
        for copy in copies:
            copy.wait_send()
    for copy in part_copies + g_copies + sq_copies + early + forwards + [own, sq_mate]:
        copy.wait_send()
    for store in stores:
        store.wait()


def exchange(n_tp, mask, x, dy, w, m, v):
    _, _, tok, feat = x.shape
    shape = w.shape
    _, _, rows, width = shape
    depth = -(-3 * rows // 16) * 16
    tiles = width // LANE
    dma = pltpu.SemaphoreType.DMA
    hbm = pl.BlockSpec(memory_space=pl.ANY)
    many = (max(n_tp - 1, 1),)
    flat = (3 * rows * tiles, LANE)
    out = jax.ShapeDtypeStruct(flat, F32)
    new = pl.pallas_call(
        functools.partial(kernel, n_tp, mask, rows, width),
        name="gossip_step",
        out_shape=(out, out, out),
        in_specs=[hbm] * 5,
        out_specs=(hbm, hbm, hbm),
        scratch_shapes=[
            pltpu.VMEM((2 * tok, feat), BF16),
            pltpu.VMEM((3, depth * tiles, LANE), F32),
            pltpu.VMEM((3, depth, width), BF16),
            pltpu.VMEM((3, depth, width), BF16),
            pltpu.VMEM((n_tp, depth, feat), BF16),
            pltpu.VMEM((n_tp, n_tp, depth, tok), F32),
            pltpu.VMEM((n_tp, depth, tok), F32),
            pltpu.VMEM((n_tp, depth, tok), F32),
            pltpu.VMEM((n_tp, depth, feat), BF16),
            pltpu.VMEM((depth, width), BF16),
            pltpu.VMEM((depth, width), BF16),
            pltpu.VMEM((8, LANE), F32),
            pltpu.VMEM((n_tp, 8, LANE), F32),
            pltpu.VMEM((8, LANE), F32),
            pltpu.VMEM((8, LANE), F32),
            dma((5,)),
            dma((3,)),
            dma(many), dma(many),
            dma(many), dma(many),
            dma(many), dma(many),
            dma(many), dma(many),
            dma((3,)), dma((3,)),
            dma((n_tp,)), dma((n_tp,)),
            dma((1,)), dma((1,)),
            dma((3, n_tp)), dma((3, n_tp)),
        ],
        compiler_params=pltpu.CompilerParams(
            collective_id=mask, has_side_effects=True, vmem_limit_bytes=VMEM_LIMIT
        ),
    )(x, dy, *(value.reshape(flat) for value in (w, m, v)))
    return new


def place(*refs):
    copies = [
        pltpu.make_async_copy(refs[k], refs[3 + k], refs[6].at[k]) for k in range(3)
    ]
    for copy in copies:
        copy.start()
    for copy in copies:
        copy.wait()


def placed(arrays):
    hbm = pl.BlockSpec(memory_space=pl.ANY)
    return pl.pallas_call(
        place,
        name="place",
        out_shape=tuple(jax.ShapeDtypeStruct(value.shape, value.dtype) for value in arrays),
        in_specs=[hbm] * 3,
        out_specs=(hbm,) * 3,
        scratch_shapes=[pltpu.SemaphoreType.DMA((3,))],
    )(*arrays)


def solution(mesh):
    n_rep = mesh.shape["rep"]
    n_tp = mesh.shape["tp"]

    def per_device(inputs, out_grads, weights, first_moment, second_moment, partners):
        branches = [functools.partial(exchange, n_tp, mask) for mask in range(1, n_rep)]
        new = lax.switch(
            partners[0, 0] - 1, branches,
            inputs, out_grads, weights, first_moment, second_moment,
        )
        return tuple(value.reshape(weights.shape) for value in placed(new))

    return jax.shard_map(
        per_device,
        mesh=mesh,
        in_specs=(
            P("rep", None, None, "tp"),
            P("rep", None, None, "tp"),
            P("rep", None, "tp", None),
            P("rep", None, "tp", None),
            P("rep", None, "tp", None),
            P(),
        ),
        out_specs=(
            P("rep", None, "tp", None),
            P("rep", None, "tp", None),
            P("rep", None, "tp", None),
        ),
        check_vma=False,
    )
```
